128 devices in a mesh: pipe: 16 (over y_lo, x, core), tensor: 8 (over y_hi, z).
Axes of the slice: x: 4, y: 4 (y_hi: 2, y_lo: 2; y = y_hi * 2 + y_lo), z: 4, core: 2. Of those that a mesh axis runs over, the one named last changes fastest.
Arguments:
- stream: bfloat16 [16, 256, 12288], P('pipe', None, 'tensor'), may hold values from -6 to 6
- entering: bfloat16 [1, 256, 12288], P(None, None, 'tensor'), may hold values from -6 to 6
- gains: float32 [16, 12288], P('pipe'), may hold values from 0.1 to 1.9
- keys: bfloat16 [2, 16, 256, 6144], P(None, 'pipe', None, 'tensor')
- values: bfloat16 [2, 16, 256, 6144], P(None, 'pipe', None, 'tensor'), may hold values from -6 to 6
- out_weight: bfloat16 [16, 6144, 12288], P('pipe', 'tensor'), may hold values from -0.078125 to 0.078125
Outputs:
- outputs: bfloat16 [2, 16, 256, 12288], P(None, 'pipe', None, 'tensor')
The draws below stay inside these ranges and needn't reach their ends.
All inputs are finite; a program needn't handle non-finite values.
Results may differ from the reference program's by a relative error of at most 0.04.
Values may be sent and summed in bfloat16 or wider, within the bound.
A program may use at most 128 MiB of HBM per device.

```python
import jax
import jax.numpy as jnp
from jax import lax

D = 12288
HEAD_DIM = 128
HEADS = 48
TOK = 256
TICKS = 2
HW = 6144
SECTIONS = 16
N_TENSOR = 8


def draw_keys(key, part):
    key = jax.random.fold_in(key, 7)
    first = jax.random.fold_in(key, 0)
    base = jax.random.normal(first, (TICKS, SECTIONS, TOK, HW), jnp.float32)
    return base.astype(jnp.bfloat16)


def levels(rng, dims, cuts, least, high):
    factor_of, own = 1.0, jax.random.fold_in(rng, 6)
    for dim, shards_of in cuts:
        draws = jnp.exp(jax.random.uniform(jax.random.fold_in(own, dim), (shards_of,), jnp.float32, least / len(cuts), high / len(cuts)))
        factor_of = factor_of * jnp.repeat(draws, dims[dim] // shards_of).reshape([-1 if axis == dim else 1 for axis in range(len(dims))])
    return factor_of


def normal_values(key, extent, scale, bound, cuts=(), held_as=jnp.bfloat16):
    level = levels(key, extent, cuts, -0.22, 0.18) if cuts else 1.0
    values = jax.random.normal(key, extent, jnp.float32) * scale * level
    return jnp.minimum(jnp.maximum(values, -bound), bound).astype(held_as)


def setup_inputs(seed: int = 0) -> dict:
    key_list = jax.random.split(jax.random.key(seed), 7)
    stream = normal_values(key_list[0], (SECTIONS, TOK, D), 1.0, 6.0, ((0, 16), (2, 8)))
    entering = normal_values(key_list[1], (TICKS - 1, TOK, D), 1.0, 6.0, ((2, 8),))
    gains = jnp.clip(1.0 + 0.18 * jax.random.normal(key_list[2], (SECTIONS, D), jnp.float32), 0.1, 1.9)
    keys = draw_keys(jax.random.fold_in(key_list[6], 71), 0)
    values = normal_values(key_list[4], (TICKS, SECTIONS, TOK, HW), 1.0, 6.0, ((1, 16), (3, 8)))
    out_weight = normal_values(key_list[5], (SECTIONS, HW, D), HW ** -0.5, 0.078125, ((0, 16), (1, 8)))
    return dict(stream=stream, entering=entering, gains=gains, keys=keys, values=values, out_weight=out_weight)


def section_layer(operands):
    x, gain, key_rows, value_rows, weight = operands
    xf = x.astype(jnp.float32)
    center = lax.optimization_barrier(jnp.mean(xf, axis=1, keepdims=True))
    spread = lax.optimization_barrier(jnp.mean((xf - center) * (xf - center), axis=1, keepdims=True))
    normed = ((xf - center) * lax.rsqrt(spread + 1e-05) * gain[None, :]).astype(jnp.bfloat16)
    queries = normed[:, :HW].reshape(TOK, HEADS, HEAD_DIM).astype(jnp.float32)
    key_heads = key_rows.reshape(TOK, HEADS, HEAD_DIM).astype(jnp.float32)
    value_heads = value_rows.reshape(TOK, HEADS, HEAD_DIM).astype(jnp.float32)
    scores = jnp.einsum('thd,uhd->htu', queries, key_heads) / jnp.sqrt(jnp.float32(HEAD_DIM))
    rows_at = jnp.arange(TOK, dtype=jnp.int32)
    causal = rows_at[None, :, None] >= rows_at[None, None, :]
    scores = jnp.where(causal, scores, jnp.float32(-1e+30))
    top = lax.optimization_barrier(jnp.max(scores, axis=2, keepdims=True))
    expo = jnp.exp(scores - top)
    probs = (expo / lax.optimization_barrier(jnp.sum(expo, axis=2, keepdims=True))).astype(jnp.bfloat16)
    context = jnp.einsum('htu,uhd->thd', probs.astype(jnp.float32), value_heads).astype(jnp.bfloat16)
    grouped = context.reshape(TOK, N_TENSOR, HW // N_TENSOR).astype(jnp.float32)
    weight_groups = weight.reshape(N_TENSOR, HW // N_TENSOR, D).astype(jnp.float32)
    pieces = jnp.einsum('tgc,gcd->gtd', grouped, weight_groups).astype(jnp.bfloat16)
    pieces = lax.optimization_barrier(pieces)
    projected = lax.optimization_barrier(jnp.sum(pieces.astype(jnp.float32), axis=0))
    return (xf + projected).astype(jnp.bfloat16)

def reference(stream, entering, gains, keys, values, out_weight):
    results = []
    inputs = stream
    for tick in range(TICKS):
        if tick > 0:
            inputs = jnp.concatenate([entering[tick - 1][None], previous[:-1]], axis=0)
        previous = lax.map(section_layer, (inputs, gains, keys[tick], values[tick], out_weight))
        results.append(previous)
    return jnp.stack(results)
```

```python
import functools

import jax
import jax.numpy as jnp
from jax import lax
from jax.experimental import pallas as pl
from jax.experimental.pallas import tpu as pltpu
from jax.sharding import PartitionSpec as P

HEAD_DIM = 128
ROWS = 64
MESH = pl.DeviceIdType.MESH
F32 = jnp.float32
BF16 = jnp.bfloat16

A, B, Y = 1, 3, 4
ORDERS = ((A, B, Y), (B, Y, A), (Y, A, B))
N_ORDERS = 3
N_SENT = 7


def flipped(rank, mask):
    y, z = rank // 4, rank % 4
    low = mask % 4
    if low == 1:
        z = z + 1 - 2 * (z % 2)
    elif low == 2:
        z = (z + 2) % 4
    elif low == 3:
        z = 3 - z
    if mask >= 4:
        y = 1 - y
    return y * 4 + z


def held_masks(order):
    first, second, third = ORDERS[order]
    return (
        first ^ second ^ third,
        first ^ second,
        first ^ third,
        first,
        second ^ third,
        second,
        third,
        0,
    )


def centred(block):
    total = jnp.sum(block, axis=1, keepdims=True)
    off = block - total / block.shape[1]
    return total, jnp.sum(off * off, axis=1, keepdims=True)


def as_rows(total, squares):
    rows = total.shape[0]
    lane = lax.broadcasted_iota(jnp.int32, (rows, 128), 1)
    both = jnp.where(lane == 0, total, jnp.where(lane == 1, squares, 0.0))
    if rows < 128:
        both = jnp.concatenate([both, jnp.zeros((128 - rows, 128), F32)], axis=0)
    return both.T[0:8]


def kernel(
    sizes, stream, entering, gains, keys, values, weight, out,
    w_held, k_held, v_held, x_held, q_held, gain_held, enter_held, ctx, sent, got, result, relay, stat_mine, stat_all,
    w_sem, load_sem, got_sem, sent_sem, stat_sem, stat_sent, q_sem, q_sent, x_sem, x_sent, out_sem,
):
    n_pipe, ticks, tokens, width, piece = sizes
    rows = ROWS
    chunks = tokens // rows
    units = ticks * chunks
    third = piece // N_ORDERS
    heads = width // HEAD_DIM
    features = piece * 8
    section, rank = lax.axis_index("pipe"), lax.axis_index("tensor")
    after, before = (section + 1) % n_pipe, (section + n_pipe - 1) % n_pipe

    x_load = pltpu.make_async_copy(stream.at[0], x_held.at[0], load_sem.at[0])
    x_load.start()
    w_loads = []
    loads = [
        pltpu.make_async_copy(
            gains.at[:, pl.ds(pl.multiple_of(rank * width, 128), width)], gain_held, load_sem.at[1]
        ),
        pltpu.make_async_copy(keys.at[:, 0], k_held, load_sem.at[2]),
        pltpu.make_async_copy(values.at[:, 0], v_held, load_sem.at[3]),
    ]
    for copy in loads:
        copy.start()
    for place in range(8):
        for order in range(N_ORDERS):
            owner = flipped(rank, held_masks(order)[place])
            start = pl.multiple_of(owner * piece + order * third, 128)
            copy = pltpu.make_async_copy(
                weight.at[0, :, pl.ds(start, third)],
                w_held.at[place * N_ORDERS + order],
                w_sem.at[place * N_ORDERS + order],
            )
            copy.start()
            w_loads.append(copy)
    enter_load = pltpu.make_async_copy(entering.at[0], enter_held, load_sem.at[4])
    enter_load.start()

    barrier = pltpu.get_barrier_semaphore()
    for peer in range(8):
        pl.semaphore_signal(barrier, inc=1, device_id=(before, peer), device_id_type=MESH)
    for mask in range(1, 8):
        pl.semaphore_signal(
            barrier, inc=1, device_id=(section, flipped(rank, mask)), device_id_type=MESH
        )
    pl.semaphore_wait(barrier, 15)

    def query_rows(chunk):
        return pl.ds(pl.multiple_of(chunk * rows, rows), rows)

    @pl.when(rank < 4)
    def _():
        for chunk in range(chunks):
            for half in range(2):
                source = stream.at[0, query_rows(chunk), pl.ds(half * width, width)]
                target = q_held.at[0, query_rows(chunk)]

                def far(source=source, target=target, half=half, chunk=chunk):
                    pltpu.make_async_remote_copy(
                        source, target, q_sent.at[0, half], q_sem.at[chunk],
                        device_id=(section, 2 * rank + half), device_id_type=MESH,
                    ).start()

                if half == 0:

                    @pl.when(rank == 0)
                    def _(source=source, target=target, chunk=chunk):
                        pltpu.make_async_copy(source, target, q_sem.at[chunk]).start()

                    pl.when(rank > 0)(far)
                else:
                    far()

    x_load.wait()
    for chunk in range(chunks):
        block = x_held[0, chunk * rows : (chunk + 1) * rows, :].astype(F32)
        line = as_rows(*centred(block))
        stat_mine[chunk] = line
        stat_all[rank, chunk] = line
    for mask in range(1, 8):
        pltpu.make_async_remote_copy(
            stat_mine.at[pl.ds(0, chunks)],
            stat_all.at[rank, pl.ds(0, chunks)],
            stat_sent.at[0],
            stat_sem.at[0, rank],
            device_id=(section, flipped(rank, mask)),
            device_id_type=MESH,
        ).start()
    for copy in loads:
        copy.wait()

    def hop(unit, slot, mask):
        return pltpu.make_async_remote_copy(
            sent.at[unit, slot],
            got.at[unit, slot],
            sent_sem.at[unit],
            got_sem.at[unit, slot],
            device_id=(section, flipped(rank, mask)),
            device_id_type=MESH,
        )

    def product(unit, place, order):
        return jnp.dot(
            ctx[unit], w_held[place * N_ORDERS + order], preferred_element_type=F32
        )

    def arrived(unit, slot):
        hop(unit, slot, A).wait_recv()
        return got[unit, slot].astype(F32)

    def have(unit, slot):
        return got[unit, slot].astype(F32)

    def slot_of(order, place):
        return place * N_ORDERS + order

    def attend(unit):
        tick, chunk = unit // chunks, unit % chunks
        at = query_rows(chunk)

        @pl.when(unit == 0)
        def _():
            for mask in range(1, 8):
                peer = flipped(rank, mask)
                pltpu.make_async_remote_copy(
                    stat_mine.at[pl.ds(0, chunks)], stat_all.at[peer, pl.ds(0, chunks)],
                    stat_sent.at[0], stat_sem.at[0, peer], device_id=(section, peer), device_id_type=MESH,
                ).wait_recv()

        @pl.when(tick > 0)
        def _():
            for peer in range(8):
                pltpu.make_async_remote_copy(
                    stat_mine.at[unit], stat_all.at[peer, unit],
                    stat_sent.at[1], stat_sem.at[1 + chunk, peer], device_id=(after, peer), device_id_type=MESH,
                ).wait_recv()

        pltpu.make_async_remote_copy(
            q_held.at[tick, at], q_held.at[tick, at], q_sent.at[0, 0], q_sem.at[unit],
            device_id=(after, rank), device_id_type=MESH,
        ).wait_recv()

        lines = [stat_all[peer, unit] for peer in range(8)]
        mean = sum(line[0:1] for line in lines) / features
        spread = sum(
            line[1:2] + (line[0:1] / piece - mean) * (line[0:1] / piece - mean) * piece
            for line in lines
        )
        scale = lax.rsqrt(spread / features + 1e-05)
        mean = jnp.broadcast_to(mean, (128, 128)).T[0:rows]
        scale = jnp.broadcast_to(scale, (128, 128)).T[0:rows]
        row = lax.broadcasted_iota(jnp.int32, (rows, tokens), 0) + chunk * rows
        column = lax.broadcasted_iota(jnp.int32, (rows, tokens), 1)
        causal = row >= column
        for head in range(heads):
            span = slice(head * HEAD_DIM, (head + 1) * HEAD_DIM)
            raw = q_held[tick, at, span].astype(F32)
            query = ((raw - mean) * scale * gain_held[0:1, span]).astype(BF16)
            scores = lax.dot_general(
                query, k_held[tick, :, span], (((1,), (1,)), ((), ())), preferred_element_type=F32
            )
            scores = jnp.where(causal, scores * (HEAD_DIM**-0.5), -1e30)
            expo = jnp.exp(scores - jnp.max(scores, axis=1, keepdims=True))
            probs = (expo * (1.0 / jnp.sum(expo, axis=1, keepdims=True))).astype(BF16)
            mixed = jnp.dot(probs, v_held[tick, :, span], preferred_element_type=F32)
            ctx[unit, :, span] = mixed.astype(BF16)

        for place in range(4):
            for order in range(N_ORDERS):

                @pl.when(unit == 0)
                def _(place=place, order=order):
                    w_loads[place * N_ORDERS + order].wait()

                slot = slot_of(order, place)
                sent[unit, slot] = product(unit, place, order).astype(BF16)
                hop(unit, slot, ORDERS[order][0]).start()

    def second(unit):
        for place in (4, 5):
            for order in range(N_ORDERS):

                @pl.when(unit == 0)
                def _(place=place, order=order):
                    w_loads[place * N_ORDERS + order].wait()

                slot = slot_of(order, place)
                value = product(unit, place, order) + arrived(unit, slot_of(order, place - 4))
                sent[unit, slot] = value.astype(BF16)
                hop(unit, slot, ORDERS[order][1]).start()

    def last(unit):
        for order in range(N_ORDERS):

            @pl.when(unit == 0)
            def _(order=order):
                w_loads[6 * N_ORDERS + order].wait()

            slot = slot_of(order, 6)
            value = product(unit, 6, order) + arrived(unit, slot_of(order, 2))
            value = value + arrived(unit, slot_of(order, 4))
            sent[unit, slot] = value.astype(BF16)
            hop(unit, slot, ORDERS[order][2]).start()

    def relay_x(chunk):
        return pltpu.make_async_remote_copy(
            relay.at[chunk], x_held.at[1, query_rows(chunk)], x_sent.at[0], x_sem.at[chunk],
            device_id=(after, rank), device_id_type=MESH,
        )

    def finish(unit):
        tick, chunk = unit // chunks, unit % chunks
        at = query_rows(chunk)

        @pl.when(unit == 0)
        def _():
            enter_load.wait()
            for order in range(N_ORDERS):
                w_loads[7 * N_ORDERS + order].wait()

        @pl.when(tick > 0)
        def _():
            relay_x(chunk).wait_recv()

        for order in range(N_ORDERS):
            span = slice(order * third, (order + 1) * third)
            value = product(unit, 7, order) + x_held[tick, at, span].astype(F32)
            for place in (3, 5, 6):
                value = value + arrived(unit, slot_of(order, place))
            result[unit, :, span] = value.astype(BF16)
        pltpu.make_async_copy(result.at[unit], out.at[tick, 0, at], out_sem.at[unit]).start()

        @pl.when(tick == 0)
        def _():
            @pl.when(section == n_pipe - 1)
            def _():
                relay[chunk] = enter_held[at]

            @pl.when(section < n_pipe - 1)
            def _():
                relay[chunk] = result[unit]

            stat_mine[chunks + chunk] = as_rows(*centred(relay[chunk].astype(F32)))
            for peer in range(8):
                pltpu.make_async_remote_copy(
                    stat_mine.at[chunks + chunk], stat_all.at[rank, chunks + chunk],
                    stat_sent.at[1], stat_sem.at[1 + chunk, rank], device_id=(after, peer), device_id_type=MESH,
                ).start()

            @pl.when(rank < 4)
            def _():
                for half in range(2):
                    pltpu.make_async_remote_copy(
                        relay.at[chunk, :, pl.ds(half * width, width)], q_held.at[1, at],
                        q_sent.at[1, half], q_sem.at[chunks + chunk],
                        device_id=(after, 2 * rank + half), device_id_type=MESH,
                    ).start()

            relay_x(chunk).start()

    def step(i, carry):
        pl.when(i < units)(lambda: attend(i))
        pl.when(i >= 3)(lambda: finish(i - 3))
        pl.when((i >= 2) & (i < units + 2))(lambda: last(i - 2))
        pl.when((i >= 1) & (i < units + 1))(lambda: second(i - 1))
        return carry

    lax.fori_loop(0, units + 3, step, 0)

    for unit in range(units):
        pltpu.make_async_remote_copy(
            sent.at[unit], got.at[unit], sent_sem.at[unit], got_sem.at[unit, 0],
            device_id=(section, flipped(rank, A)), device_id_type=MESH,
        ).wait_send()
        tick, chunk = divmod(unit, chunks)
        pltpu.make_async_copy(
            result.at[unit], out.at[tick, 0, query_rows(chunk)], out_sem.at[unit]
        ).wait()
    pltpu.make_async_remote_copy(
        stat_all.at[pl.ds(0, 7), pl.ds(0, chunks)], stat_all.at[pl.ds(0, 7), pl.ds(0, chunks)],
        stat_sent.at[0], stat_sem.at[0, 0], device_id=(after, rank), device_id_type=MESH,
    ).wait_send()
    pltpu.make_async_remote_copy(
        stat_all.at[:, pl.ds(0, chunks)], stat_all.at[:, pl.ds(0, chunks)],
        stat_sent.at[1], stat_sem.at[0, 0], device_id=(after, rank), device_id_type=MESH,
    ).wait_send()
    pltpu.make_async_remote_copy(
        x_held.at[1], x_held.at[1], x_sent.at[0], x_sem.at[0], device_id=(after, rank), device_id_type=MESH
    ).wait_send()

    def queries_sent(tick, half):
        pltpu.make_async_remote_copy(
            q_held.at[tick], q_held.at[tick], q_sent.at[tick, half], q_sem.at[0],
            device_id=(after, rank), device_id_type=MESH,
        ).wait_send()

    @pl.when(rank < 4)
    def _():
        pl.when(rank > 0)(lambda: queries_sent(0, 0))
        queries_sent(0, 1)
        queries_sent(1, 0)
        queries_sent(1, 1)


def body(n_pipe, stream, entering, gains, keys, values, weight):
    ticks, _, tokens, width = keys.shape
    piece = stream.shape[2]
    third = piece // N_ORDERS
    chunks = tokens // ROWS
    units = ticks * chunks
    vmem, dma = pltpu.VMEM, pltpu.SemaphoreType.DMA
    anywhere = pl.BlockSpec(memory_space=pl.ANY)
    return pl.pallas_call(
        functools.partial(kernel, (n_pipe, ticks, tokens, width, piece)),
        out_shape=jax.ShapeDtypeStruct((ticks, 1, tokens, piece), BF16),
        in_specs=[anywhere] * 6,
        out_specs=anywhere,
        scratch_shapes=[
            vmem((8 * N_ORDERS, width, third), BF16),
            vmem((ticks, tokens, width), BF16),
            vmem((ticks, tokens, width), BF16),
            vmem((ticks, tokens, piece), BF16),
            vmem((ticks, tokens, width), BF16),
            vmem((1, width), F32),
            vmem((tokens, piece), BF16),
            vmem((units, ROWS, width), BF16),
            vmem((units, N_SENT * N_ORDERS, ROWS, third), BF16),
            vmem((units, N_SENT * N_ORDERS, ROWS, third), BF16),
            vmem((units, ROWS, piece), BF16),
            vmem((chunks, ROWS, piece), BF16),
            vmem((units, 8, 128), F32),
            vmem((8, units, 8, 128), F32),
            dma((8 * N_ORDERS,)),
            dma((5,)),
            dma((units, N_SENT * N_ORDERS)),
            dma((units,)),
            dma((1 + chunks, 8)),
            dma((2,)),
            dma((units,)),
            dma((2, 2)),
            dma((chunks,)),
            dma((1,)),
            dma((units,)),
        ],
        compiler_params=pltpu.CompilerParams(
            collective_id=0, has_side_effects=True, vmem_limit_bytes=58 * 2**20
        ),
        name="relay",
    )(stream, entering, gains, keys, values, weight)


def solution(mesh):
    in_specs = (
        P("pipe", None, "tensor"),
        P(None, None, "tensor"),
        P("pipe", None),
        P(None, "pipe", None, "tensor"),
        P(None, "pipe", None, "tensor"),
        P("pipe", "tensor", None),
    )
    out_specs = P(None, "pipe", None, "tensor")
    return jax.shard_map(
        functools.partial(body, mesh.shape["pipe"]),
        mesh=mesh, in_specs=in_specs, out_specs=out_specs, check_vma=False,
    )
```

```python
import functools

import jax
import jax.numpy as jnp
from jax import lax
from jax.experimental import pallas as pl
from jax.experimental.pallas import tpu as pltpu
from jax.sharding import PartitionSpec as P

HEAD_DIM = 128
PARTS = (64, 64, 128)
MESH = pl.DeviceIdType.MESH
F32 = jnp.float32
BF16 = jnp.bfloat16

A, B, Y = 1, 3, 4
ORDERS = ((A, B, Y), (B, Y, A), (Y, A, B))
N_ORDERS = 3
N_SENT = 7


def flipped(rank, mask):
    y, z = rank // 4, rank % 4
    low = mask % 4
    if low == 1:
        z = z + 1 - 2 * (z % 2)
    elif low == 2:
        z = (z + 2) % 4
    elif low == 3:
        z = 3 - z
    if mask >= 4:
        y = 1 - y
    return y * 4 + z


def held_masks(order):
    first, second, third = ORDERS[order]
    return (
        first ^ second ^ third,
        first ^ second,
        first ^ third,
        first,
        second ^ third,
        second,
        third,
        0,
    )


def centred(block):
    total = jnp.sum(block, axis=1, keepdims=True)
    off = block - total / block.shape[1]
    return total, jnp.sum(off * off, axis=1, keepdims=True)


def as_rows(total, squares):
    rows = total.shape[0]
    lane = lax.broadcasted_iota(jnp.int32, (rows, 128), 1)
    both = jnp.where(lane == 0, total, jnp.where(lane == 1, squares, 0.0))
    if rows < 128:
        both = jnp.concatenate([both, jnp.zeros((128 - rows, 128), F32)], axis=0)
    return both.T[0:8]


PLAN = (
    "a0", "p00", "p01", "w1", "p02", "p03", "s04", "s05", "a1", "w2", "p10", "p11", "l0", "p12", "p13", "f0",
    "a2", "p20", "s14", "s15", "p21", "x3", "p22", "p23", "w3", "l1", "f1", "s24", "s25", "a3", "p30", "t1",
    "p31", "x4", "l2", "p32", "p33", "w4", "f2", "a4", "p40", "p41", "s34", "s35", "t2", "p42", "p43", "x5",
    "s44", "s45", "l3", "w5", "a5", "p50", "p51", "l4", "p52", "p53", "f3", "s54", "s55", "f4", "l5", "f5",
)
ROUND = ((13, 1, 64), (15, 2, 128), (11, 2, 192))
ROUND_ROWS = 64


def kernel(
    sizes, stream, entering, gains, keys, values, weight, out,
    w_held, k_held, v_held, x_held, q_held, pass_held, gain_held, ctx, sent, got, turn_held, stat_mine, stat_all,
    w_sem, load_sem, got_sem, sent_sem, stat_sem, stat_sent, q_sem, q_sent, pass_sem, pass_sent, x_sem, x_sent, turn_sem, turn_sent,
):
    n_pipe, ticks, tokens, width, piece = sizes
    n = len(PARTS)
    first_row = [sum(PARTS[:i]) for i in range(n)]
    third = piece // N_ORDERS
    heads = width // HEAD_DIM
    features = piece * 8
    section, rank = lax.axis_index("pipe"), lax.axis_index("tensor")
    after, before = (section + 1) % n_pipe, (section + n_pipe - 1) % n_pipe

    def span_of(part):
        return pl.ds(first_row[part], PARTS[part])

    def both_of(unit):
        tick, part = divmod(unit, n)
        return pl.ds(tick * tokens + first_row[part], PARTS[part])

    def remote(source, target, send, receive, where):
        return pltpu.make_async_remote_copy(
            source, target, send, receive, device_id=where, device_id_type=MESH
        )

    barrier = pltpu.get_barrier_semaphore()
    for mask in range(1, 8):
        pl.semaphore_signal(
            barrier, inc=1, device_id=(section, flipped(rank, mask)), device_id_type=MESH
        )
    pl.semaphore_signal(barrier, inc=1, device_id=(before, rank), device_id_type=MESH)
    for turn, _, _ in ROUND:

        @pl.when(section == turn)
        def _():
            pl.semaphore_signal(barrier, inc=1, device_id=(7, rank), device_id_type=MESH)

        @pl.when(section == 8)
        def _(turn=turn):
            pl.semaphore_signal(barrier, inc=1, device_id=(turn, rank), device_id_type=MESH)


    x_load = pltpu.make_async_copy(stream.at[0], x_held.at[0], load_sem.at[0])
    x_load.start()
    w_loads = []
    loads = [
        pltpu.make_async_copy(
            gains.at[:, pl.ds(pl.multiple_of(rank * width, 128), width)], gain_held, load_sem.at[1]
        ),
        pltpu.make_async_copy(keys.at[:, 0], k_held, load_sem.at[2]),
        pltpu.make_async_copy(values.at[:, 0], v_held, load_sem.at[3]),
    ]
    for copy in loads:
        copy.start()
    for place in range(8):
        for order in range(N_ORDERS):
            owner = flipped(rank, held_masks(order)[place])
            start = pl.multiple_of(owner * piece + order * third, 128)
            w_loads.append(
                pltpu.make_async_copy(
                    weight.at[0, :, pl.ds(start, third)],
                    w_held.at[place * N_ORDERS + order],
                    w_sem.at[place * N_ORDERS + order],
                )
            )
    early = 2 * N_ORDERS
    for copy in w_loads[:early]:
        copy.start()

    enter_load = pltpu.make_async_copy(entering.at[0], x_held.at[1], load_sem.at[4])

    def query_send(tick, part, half):
        unit, at = tick * n + part, span_of(part)
        direct = tick == 0 and part == 0
        passed = (rank >= 2) if half == 0 else (rank == 2)
        target = 2 * rank + half
        source = x_held.at[tick, at, pl.ds(half * width, width)]

        def far():
            remote(
                source, q_held.at[tick, at], q_sent.at[tick, half], q_sem.at[unit], (section, target)
            ).start()

        def near():
            remote(
                source, pass_held.at[tick, at], q_sent.at[tick, half], pass_sem.at[unit], (section, target - 4)
            ).start()

        def own():
            pltpu.make_async_copy(source, q_held.at[tick, at], q_sem.at[unit]).start()

        away = (rank > 0) if half == 0 else (rank >= 0)
        if half == 0:
            pl.when(rank == 0)(own)
        if direct:
            pl.when(away)(far)
        else:
            pl.when(passed)(near)
            pl.when(away & (rank < 2) if half == 0 else (rank != 2))(far)

    def pass_on(unit):
        tick, part = divmod(unit, n)
        at = span_of(part)

        @pl.when(rank < 3)
        def _():
            copy = remote(
                pass_held.at[tick, at], pass_held.at[tick, at], q_sent.at[0, 0], pass_sem.at[unit], (after, rank)
            )
            copy.wait_recv()
            remote(
                pass_held.at[tick, at], q_held.at[tick, at], pass_sent.at[tick], q_sem.at[unit],
                (section, rank + 4),
            ).start()

    def measure(unit):
        tick, part = divmod(unit, n)
        line = as_rows(*centred(x_held[tick, span_of(part), :].astype(F32)))
        stat_mine[unit] = line
        stat_all[rank, unit] = line

    def distribute(unit):
        tick, part = divmod(unit, n)
        for mask in range(1, 8):
            remote(
                stat_mine.at[unit], stat_all.at[rank, unit], stat_sent.at[0], stat_sem.at[unit, rank],
                (section, flipped(rank, mask)),
            ).start()

        @pl.when(rank < 4)
        def _():
            for half in (1, 0):
                query_send(tick, part, half)

    def take(unit):
        part = unit - n
        if part == 0:
            pl.when(section == 0)(enter_load.wait)

        @pl.when(section > 0)
        def _():
            relay_x(part).wait_recv()

        measure(unit)
        distribute(unit)

    x_load.wait()
    for part in range(n):
        measure(part)
    helps = functools.reduce(lambda a, b: a | b, [section == turn for turn, _, _ in ROUND])

    @pl.when(section == 7)
    def _():
        pl.semaphore_wait(barrier, 8 + len(ROUND))

    @pl.when(helps)
    def _():
        pl.semaphore_wait(barrier, 9)

    @pl.when((section != 7) & jnp.logical_not(helps))
    def _():
        pl.semaphore_wait(barrier, 8)

    for part in range(n):
        distribute(part)

    for copy in w_loads[early:]:
        copy.start()
    pl.when(section == 0)(enter_load.start)
    for copy in loads:
        copy.wait()

    def hop(unit, slot, mask):
        at = both_of(unit)
        return remote(
            sent.at[slot, at], got.at[slot, at], sent_sem.at[slot], got_sem.at[unit, slot],
            (section, flipped(rank, mask)),
        )

    def product(unit, place, order):
        if unit == 0:
            w_loads[place * N_ORDERS + order].wait()
        return jnp.dot(
            ctx[both_of(unit), :], w_held[place * N_ORDERS + order], preferred_element_type=F32
        )

    def arrived(unit, slot):
        hop(unit, slot, A).wait_recv()
        return got[slot, both_of(unit), :].astype(F32)

    def slot_of(order, place):
        return place * N_ORDERS + order

    def attend(unit):
        tick, part = divmod(unit, n)
        rows = PARTS[part]
        for mask in range(1, 8):
            peer = flipped(rank, mask)
            remote(
                stat_mine.at[unit], stat_all.at[peer, unit], stat_sent.at[0], stat_sem.at[unit, peer],
                (section, peer),
            ).wait_recv()
        lines = [stat_all[peer, unit] for peer in range(8)]
        mean = sum(line[0:1] for line in lines) / features
        spread = sum(
            line[1:2] + (line[0:1] / piece - mean) * (line[0:1] / piece - mean) * piece
            for line in lines
        )
        scale = lax.rsqrt(spread / features + 1e-05)
        mean = jnp.broadcast_to(mean, (128, 128)).T[0:rows]
        scale = jnp.broadcast_to(scale, (128, 128)).T[0:rows]
        row = lax.broadcasted_iota(jnp.int32, (rows, tokens), 0) + first_row[part]
        column = lax.broadcasted_iota(jnp.int32, (rows, tokens), 1)
        causal = row >= column
        remote(
            q_held.at[tick, span_of(part)], q_held.at[tick, span_of(part)], q_sent.at[0, 0], q_sem.at[unit],
            (after, rank),
        ).wait_recv()
        spans = [slice(head * HEAD_DIM, (head + 1) * HEAD_DIM) for head in range(heads)]
        scores = []
        for span in spans:
            raw = q_held[tick, span_of(part), span].astype(F32)
            query = ((raw - mean) * scale * gain_held[0:1, span]).astype(BF16)
            scores.append(
                lax.dot_general(
                    query, k_held[tick, :, span], (((1,), (1,)), ((), ())), preferred_element_type=F32
                )
            )
        probs = []
        for score in scores:
            score = jnp.where(causal, score * (HEAD_DIM**-0.5), -1e30)
            expo = jnp.exp(score - jnp.max(score, axis=1, keepdims=True))
            probs.append((expo * (1.0 / jnp.sum(expo, axis=1, keepdims=True))).astype(BF16))
        mixed = [
            jnp.dot(prob, v_held[tick, :, span], preferred_element_type=F32).astype(BF16)
            for prob, span in zip(probs, spans)
        ]
        for value, span in zip(mixed, spans):
            ctx[both_of(unit), span] = value

    def send(unit, place, stage, values):
        for order in range(N_ORDERS):
            sent[slot_of(order, place), both_of(unit), :] = values[order].astype(BF16)
        for order in range(N_ORDERS):
            hop(unit, slot_of(order, place), ORDERS[order][stage]).start()

    def first(unit, place):
        send(unit, place, 0, [product(unit, place, order) for order in range(N_ORDERS)])

    def second(unit, place):
        values = [
            product(unit, place, order) + arrived(unit, slot_of(order, place - 4))
            for order in range(N_ORDERS)
        ]
        send(unit, place, 1, values)

    def last(unit):
        values = [
            product(unit, 6, order) + arrived(unit, slot_of(order, 2)) + arrived(unit, slot_of(order, 4))
            for order in range(N_ORDERS)
        ]
        send(unit, 6, 2, values)

    def relay_x(part):
        return remote(
            out.at[0, 0, span_of(part)], x_held.at[1, span_of(part)], x_sent.at[0], x_sem.at[part], (after, rank)
        )

    def turn_in(turn, row):
        return remote(
            out.at[0, 0, pl.ds(row, ROUND_ROWS)], turn_held, x_sent.at[0], turn_sem.at[0], (turn, rank)
        )

    def turn_out(part, row):
        return remote(
            turn_held, x_held.at[1, pl.ds(row, ROUND_ROWS)], turn_sent.at[0], x_sem.at[part], (8, rank)
        )

    def pass_turn(part):
        for turn, its_part, row in ROUND:
            if its_part == part:

                @pl.when(section == turn)
                def _(turn=turn, row=row):
                    turn_in(turn, row).wait_recv()
                    turn_out(part, row).start()

    def hand_over(part):
        turns = [entry for entry in ROUND if entry[1] == part]
        if not turns:
            pl.when(section < n_pipe - 1)(relay_x(part).start)
            return
        pl.when((section < n_pipe - 1) & (section != 7))(relay_x(part).start)

        @pl.when(section == 7)
        def _():
            for turn, _, row in turns:
                turn_in(turn, row).start()

    def finish(unit):
        tick, part = divmod(unit, n)
        at = span_of(part)
        values = []
        for order in range(N_ORDERS):
            span = slice(order * third, (order + 1) * third)
            value = product(unit, 7, order) + x_held[tick, at, span].astype(F32)
            for place in (3, 5, 6):
                value = value + arrived(unit, slot_of(order, place))
            values.append(value.astype(BF16))
        for order in range(N_ORDERS):
            out[tick, 0, at, order * third : (order + 1) * third] = values[order]
        if tick == 0:
            hand_over(part)

    work = {"x": take, "a": attend, "p": first, "s": second, "l": last, "f": finish, "w": pass_on, "t": pass_turn}
    for item in PLAN:
        work[item[0]](*(int(digit) for digit in item[1:]))

    for slot in range(N_SENT * N_ORDERS):
        remote(
            sent.at[slot], got.at[slot], sent_sem.at[slot], got_sem.at[0, 0], (section, flipped(rank, A))
        ).wait_send()
    some = stat_all.at[pl.ds(0, 7)]
    remote(some, some, stat_sent.at[0], stat_sem.at[0, 0], (after, rank)).wait_send()

    for turn, part, row in ROUND:
        pl.when(section == turn)(turn_out(part, row).wait_send)

    @pl.when(section < n_pipe - 1)
    def _():
        remote(x_held.at[1], x_held.at[1], x_sent.at[0], x_sem.at[0], (after, rank)).wait_send()

    def queries_sent(tick, half):
        remote(
            q_held.at[tick], q_held.at[tick], q_sent.at[tick, half], q_sem.at[0], (after, rank)
        ).wait_send()

    @pl.when(rank < 4)
    def _():
        for tick in range(ticks):
            pl.when(rank > 0)(functools.partial(queries_sent, tick, 0))
            queries_sent(tick, 1)

    @pl.when(rank < 3)
    def _():
        for tick in range(2):
            begun = pass_held.at[tick, pl.ds((1 - tick) * PARTS[0], tokens - (1 - tick) * PARTS[0])]
            remote(begun, begun, pass_sent.at[tick], pass_sem.at[0], (after, rank)).wait_send()


def body(n_pipe, stream, entering, gains, keys, values, weight):
    ticks, _, tokens, width = keys.shape
    piece = stream.shape[2]
    third = piece // N_ORDERS
    n = len(PARTS)
    slots = N_SENT * N_ORDERS
    vmem, dma = pltpu.VMEM, pltpu.SemaphoreType.DMA
    return pl.pallas_call(
        functools.partial(kernel, (n_pipe, ticks, tokens, width, piece)),
        out_shape=pltpu.VMEM((ticks, 1, tokens, piece), BF16),
        in_specs=[pl.BlockSpec(memory_space=pltpu.HBM)] * 6,
        out_specs=pl.BlockSpec(memory_space=pltpu.VMEM),
        scratch_shapes=[
            vmem((8 * N_ORDERS, width, third), BF16),
            vmem((ticks, tokens, width), BF16),
            vmem((ticks, tokens, width), BF16),
            vmem((ticks, tokens, piece), BF16),
            vmem((ticks, tokens, width), BF16),
            vmem((ticks, tokens, width), BF16),
            vmem((1, width), F32),
            vmem((ticks * tokens, width), BF16),
            vmem((slots, ticks * tokens, third), BF16),
            vmem((slots, ticks * tokens, third), BF16),
            vmem((ROUND_ROWS, piece), BF16),
            vmem((ticks * n, 8, 128), F32),
            vmem((8, ticks * n, 8, 128), F32),
            dma((8 * N_ORDERS,)),
            dma((5,)),
            dma((ticks * n, slots)),
            dma((slots,)),
            dma((ticks * n, 8)),
            dma((1,)),
            dma((ticks * n,)),
            dma((2, 2)),
            dma((ticks * n,)),
            dma((2,)),
            dma((n,)),
            dma((1,)),
            dma((1,)),
            dma((1,)),
        ],
        compiler_params=pltpu.CompilerParams(
            collective_id=0, has_side_effects=True, vmem_limit_bytes=52 * 2**20
        ),
        name="relay",
    )(stream, entering, gains, keys, values, weight)


def solution(mesh):
    in_specs = (
        P("pipe", None, "tensor"),
        P(None, None, "tensor"),
        P("pipe", None),
        P(None, "pipe", None, "tensor"),
        P(None, "pipe", None, "tensor"),
        P("pipe", "tensor", None),
    )
    out_specs = P(None, "pipe", None, "tensor")
    return jax.shard_map(
        functools.partial(body, mesh.shape["pipe"]),
        mesh=mesh, in_specs=in_specs, out_specs=out_specs, check_vma=False,
    )
```

```python
import functools

import jax
import jax.numpy as jnp
from jax import lax
from jax.experimental import pallas as pl
from jax.experimental.pallas import tpu as pltpu
from jax.sharding import PartitionSpec as P

HEAD_DIM = 128
PARTS = (64, 64, 128)
MESH = pl.DeviceIdType.MESH
F32 = jnp.float32
BF16 = jnp.bfloat16

A, B, Y = 1, 3, 4
ORDERS = ((A, B, Y), (B, Y, A), (Y, A, B))
N_ORDERS = 3
N_SENT = 7


def flipped(rank, mask):
    y, z = rank // 4, rank % 4
    low = mask % 4
    if low == 1:
        z = z + 1 - 2 * (z % 2)
    elif low == 2:
        z = (z + 2) % 4
    elif low == 3:
        z = 3 - z
    if mask >= 4:
        y = 1 - y
    return y * 4 + z


def held_masks(order):
    first, second, third = ORDERS[order]
    return (
        first ^ second ^ third,
        first ^ second,
        first ^ third,
        first,
        second ^ third,
        second,
        third,
        0,
    )


def centred(block):
    total = jnp.sum(block, axis=1, keepdims=True)
    off = block - total / block.shape[1]
    return total, jnp.sum(off * off, axis=1, keepdims=True)


def as_rows(total, squares):
    rows = total.shape[0]
    lane = lax.broadcasted_iota(jnp.int32, (rows, 128), 1)
    both = jnp.where(lane == 0, total, jnp.where(lane == 1, squares, 0.0))
    if rows < 128:
        both = jnp.concatenate([both, jnp.zeros((128 - rows, 128), F32)], axis=0)
    return both.T[0:8]


PLAN = (
    "a0", "p00", "p01", "w1", "p02", "p03", "s04", "s05", "a1", "w2", "p10", "p11", "l0", "p12", "p13", "f0",
    "a2", "p20", "s14", "s15", "p21", "x3", "p22", "p23", "w3", "l1", "f1", "s24", "s25", "a3", "p30", "t1",
    "p31", "x4", "l2", "p32", "p33", "w4", "f2", "a4", "p40", "p41", "s34", "s35", "t2", "p42", "p43", "x5",
    "s44", "s45", "l3", "w5", "a5", "p50", "p51", "l4", "p52", "p53", "f3", "s54", "s55", "f4", "l5", "f5",
)
ROUND = ((13, 1, 64), (15, 2, 128), (11, 2, 192))
ROUND_ROWS = 64


def kernel(
    sizes, stream, entering, gains, keys, values, weight, out,
    w_held, k_held, v_held, x_held, q_held, pass_held, gain_held, ctx, sent, got, turn_held, stat_mine, stat_all,
    w_sem, load_sem, got_sem, sent_sem, stat_sem, stat_sent, q_sem, q_sent, pass_sem, pass_sent, x_sem, x_sent, turn_sem, turn_sent,
):
    n_pipe, ticks, tokens, width, piece = sizes
    n = len(PARTS)
    first_row = [sum(PARTS[:i]) for i in range(n)]
    third = piece // N_ORDERS
    heads = width // HEAD_DIM
    features = piece * 8
    section, rank = lax.axis_index("pipe"), lax.axis_index("tensor")
    after, before = (section + 1) % n_pipe, (section + n_pipe - 1) % n_pipe

    def span_of(part):
        return pl.ds(first_row[part], PARTS[part])

    def both_of(unit):
        tick, part = divmod(unit, n)
        return pl.ds(tick * tokens + first_row[part], PARTS[part])

    def remote(source, target, send, receive, where):
        return pltpu.make_async_remote_copy(
            source, target, send, receive, device_id=where, device_id_type=MESH
        )

    barrier = pltpu.get_barrier_semaphore()
    for mask in range(1, 8):
        pl.semaphore_signal(
            barrier, inc=1, device_id=(section, flipped(rank, mask)), device_id_type=MESH
        )
    pl.semaphore_signal(barrier, inc=1, device_id=(before, rank), device_id_type=MESH)
    for turn, _, _ in ROUND:

        @pl.when(section == turn)
        def _():
            pl.semaphore_signal(barrier, inc=1, device_id=(7, rank), device_id_type=MESH)

        @pl.when(section == 8)
        def _(turn=turn):
            pl.semaphore_signal(barrier, inc=1, device_id=(turn, rank), device_id_type=MESH)


    x_load = pltpu.make_async_copy(stream.at[0], x_held.at[0], load_sem.at[0])
    x_load.start()
    w_loads = []
    loads = [
        pltpu.make_async_copy(
            gains.at[:, pl.ds(pl.multiple_of(rank * width, 128), width)], gain_held, load_sem.at[1]
        ),
        pltpu.make_async_copy(keys.at[:, 0], k_held, load_sem.at[2]),
        pltpu.make_async_copy(values.at[:, 0], v_held, load_sem.at[3]),
    ]
    for copy in loads:
        copy.start()
    for place in range(8):
        for order in range(N_ORDERS):
            owner = flipped(rank, held_masks(order)[place])
            start = pl.multiple_of(owner * piece + order * third, 128)
            w_loads.append(
                pltpu.make_async_copy(
                    weight.at[0, :, pl.ds(start, third)],
                    w_held.at[place * N_ORDERS + order],
                    w_sem.at[place * N_ORDERS + order],
                )
            )
    early = 2 * N_ORDERS
    for copy in w_loads[:early]:
        copy.start()

    enter_load = pltpu.make_async_copy(entering.at[0], x_held.at[1], load_sem.at[4])

    def query_send(tick, part, half):
        unit, at = tick * n + part, span_of(part)
        direct = tick == 0 and part == 0
        passed = (rank >= 2) if half == 0 else (rank == 2)
        target = 2 * rank + half
        source = x_held.at[tick, at, pl.ds(half * width, width)]

        def far():
            remote(
                source, q_held.at[tick, at], q_sent.at[tick, half], q_sem.at[unit], (section, target)
            ).start()

        def near():
            remote(
                source, pass_held.at[tick, at], q_sent.at[tick, half], pass_sem.at[unit], (section, target - 4)
            ).start()

        def own():
            pltpu.make_async_copy(source, q_held.at[tick, at], q_sem.at[unit]).start()

        away = (rank > 0) if half == 0 else (rank >= 0)
        if half == 0:
            pl.when(rank == 0)(own)
        if direct:
            pl.when(away)(far)
        else:
            pl.when(passed)(near)
            pl.when(away & (rank < 2) if half == 0 else (rank != 2))(far)

    def pass_on(unit):
        tick, part = divmod(unit, n)
        at = span_of(part)

        @pl.when(rank < 3)
        def _():
            copy = remote(
                pass_held.at[tick, at], pass_held.at[tick, at], q_sent.at[0, 0], pass_sem.at[unit], (after, rank)
            )
            copy.wait_recv()
            remote(
                pass_held.at[tick, at], q_held.at[tick, at], pass_sent.at[tick], q_sem.at[unit],
                (section, rank + 4),
            ).start()

    def measure(unit):
        tick, part = divmod(unit, n)
        line = as_rows(*centred(x_held[tick, span_of(part), :].astype(F32)))
        stat_mine[unit] = line
        stat_all[rank, unit] = line

    def distribute(unit):
        tick, part = divmod(unit, n)
        for mask in range(1, 8):
            remote(
                stat_mine.at[unit], stat_all.at[rank, unit], stat_sent.at[0], stat_sem.at[unit, rank],
                (section, flipped(rank, mask)),
            ).start()

        @pl.when(rank < 4)
        def _():
            for half in (1, 0):
                query_send(tick, part, half)

    def take(unit):
        part = unit - n
        if part == 0:
            pl.when(section == 0)(enter_load.wait)

        @pl.when(section > 0)
        def _():
            relay_x(part).wait_recv()

        measure(unit)
        distribute(unit)

    x_load.wait()
    for part in range(n):
        measure(part)
    helps = functools.reduce(lambda a, b: a | b, [section == turn for turn, _, _ in ROUND])

    @pl.when(section == 7)
    def _():
        pl.semaphore_wait(barrier, 8 + len(ROUND))

    @pl.when(helps)
    def _():
        pl.semaphore_wait(barrier, 9)

    @pl.when((section != 7) & jnp.logical_not(helps))
    def _():
        pl.semaphore_wait(barrier, 8)

    for part in range(n):
        distribute(part)

    for copy in w_loads[early:]:
        copy.start()
    pl.when(section == 0)(enter_load.start)
    for copy in loads:
        copy.wait()

    def hop(unit, slot, mask):
        at = both_of(unit)
        return remote(
            sent.at[slot, at], got.at[slot, at], sent_sem.at[slot], got_sem.at[unit, slot],
            (section, flipped(rank, mask)),
        )

    def product(unit, place, order):
        if unit == 0:
            w_loads[place * N_ORDERS + order].wait()
        return jnp.dot(
            ctx[both_of(unit), :], w_held[place * N_ORDERS + order], preferred_element_type=F32
        )

    def arrived(unit, slot):
        hop(unit, slot, A).wait_recv()
        return got[slot, both_of(unit), :].astype(F32)

    def slot_of(order, place):
        return place * N_ORDERS + order

    def attend(unit):
        tick, part = divmod(unit, n)
        rows = PARTS[part]
        for mask in range(1, 8):
            peer = flipped(rank, mask)
            remote(
                stat_mine.at[unit], stat_all.at[peer, unit], stat_sent.at[0], stat_sem.at[unit, peer],
                (section, peer),
            ).wait_recv()
        lines = [stat_all[peer, unit] for peer in range(8)]
        mean = sum(line[0:1] for line in lines) / features
        spread = sum(
            line[1:2] + (line[0:1] / piece - mean) * (line[0:1] / piece - mean) * piece
            for line in lines
        )
        scale = lax.rsqrt(spread / features + 1e-05)
        mean = jnp.broadcast_to(mean, (128, 128)).T[0:rows]
        scale = jnp.broadcast_to(scale, (128, 128)).T[0:rows]
        row = lax.broadcasted_iota(jnp.int32, (rows, tokens), 0) + first_row[part]
        column = lax.broadcasted_iota(jnp.int32, (rows, tokens), 1)
        causal = row >= column
        remote(
            q_held.at[tick, span_of(part)], q_held.at[tick, span_of(part)], q_sent.at[0, 0], q_sem.at[unit],
            (after, rank),
        ).wait_recv()
        spans = [slice(head * HEAD_DIM, (head + 1) * HEAD_DIM) for head in range(heads)]
        scores = []
        for span in spans:
            raw = q_held[tick, span_of(part), span].astype(F32)
            query = ((raw - mean) * scale * gain_held[0:1, span]).astype(BF16)
            scores.append(
                lax.dot_general(
                    query, k_held[tick, :, span], (((1,), (1,)), ((), ())), preferred_element_type=F32
                )
            )
        probs = []
        for score in scores:
            score = jnp.where(causal, score * (HEAD_DIM**-0.5), -1e30)
            expo = jnp.exp(score - jnp.max(score, axis=1, keepdims=True))
            probs.append((expo * (1.0 / jnp.sum(expo, axis=1, keepdims=True))).astype(BF16))
        mixed = [
            jnp.dot(prob, v_held[tick, :, span], preferred_element_type=F32).astype(BF16)
            for prob, span in zip(probs, spans)
        ]
        for value, span in zip(mixed, spans):
            ctx[both_of(unit), span] = value

    def send(unit, place, stage, values):
        for order in range(N_ORDERS):
            sent[slot_of(order, place), both_of(unit), :] = values[order].astype(BF16)
        for order in range(N_ORDERS):
            hop(unit, slot_of(order, place), ORDERS[order][stage]).start()

    def first(unit, place):
        send(unit, place, 0, [product(unit, place, order) for order in range(N_ORDERS)])

    def second(unit, place):
        values = [
            product(unit, place, order) + arrived(unit, slot_of(order, place - 4))
            for order in range(N_ORDERS)
        ]
        send(unit, place, 1, values)

    def last(unit):
        values = [
            product(unit, 6, order) + arrived(unit, slot_of(order, 2)) + arrived(unit, slot_of(order, 4))
            for order in range(N_ORDERS)
        ]
        send(unit, 6, 2, values)

    def relay_x(part):
        return remote(
            out.at[0, 0, span_of(part)], x_held.at[1, span_of(part)], x_sent.at[0], x_sem.at[part], (after, rank)
        )

    def turn_in(turn, row):
        return remote(
            out.at[0, 0, pl.ds(row, ROUND_ROWS)], turn_held, x_sent.at[0], turn_sem.at[0], (turn, rank)
        )

    def turn_out(part, row):
        return remote(
            turn_held, x_held.at[1, pl.ds(row, ROUND_ROWS)], turn_sent.at[0], x_sem.at[part], (8, rank)
        )

    def pass_turn(part):
        for turn, its_part, row in ROUND:
            if its_part == part:

                @pl.when(section == turn)
                def _(turn=turn, row=row):
                    turn_in(turn, row).wait_recv()
                    turn_out(part, row).start()

    def hand_over(part):
        turns = [entry for entry in ROUND if entry[1] == part]
        if not turns:
            pl.when(section < n_pipe - 1)(relay_x(part).start)
            return
        pl.when((section < n_pipe - 1) & (section != 7))(relay_x(part).start)

        @pl.when(section == 7)
        def _():
            for turn, _, row in turns:
                turn_in(turn, row).start()

    def finish(unit):
        tick, part = divmod(unit, n)
        at = span_of(part)
        values = []
        for order in range(N_ORDERS):
            span = slice(order * third, (order + 1) * third)
            value = product(unit, 7, order) + x_held[tick, at, span].astype(F32)
            for place in (3, 5, 6):
                value = value + arrived(unit, slot_of(order, place))
            values.append(value.astype(BF16))
        for order in range(N_ORDERS):
            out[tick, 0, at, order * third : (order + 1) * third] = values[order]
        if tick == 0:
            hand_over(part)

    work = {"x": take, "a": attend, "p": first, "s": second, "l": last, "f": finish, "w": pass_on, "t": pass_turn}
    for item in PLAN:
        work[item[0]](*(int(digit) for digit in item[1:]))

    for slot in range(N_SENT * N_ORDERS):
        remote(
            sent.at[slot], got.at[slot], sent_sem.at[slot], got_sem.at[0, 0], (section, flipped(rank, A))
        ).wait_send()
    some = stat_all.at[pl.ds(0, 7)]
    remote(some, some, stat_sent.at[0], stat_sem.at[0, 0], (after, rank)).wait_send()

    for turn, part, row in ROUND:
        pl.when(section == turn)(turn_out(part, row).wait_send)

    @pl.when(section < n_pipe - 1)
    def _():
        remote(x_held.at[1], x_held.at[1], x_sent.at[0], x_sem.at[0], (after, rank)).wait_send()

    def queries_sent(tick, half):
        remote(
            q_held.at[tick], q_held.at[tick], q_sent.at[tick, half], q_sem.at[0], (after, rank)
        ).wait_send()

    @pl.when(rank < 4)
    def _():
        for tick in range(ticks):
            pl.when(rank > 0)(functools.partial(queries_sent, tick, 0))
            queries_sent(tick, 1)

    @pl.when(rank < 3)
    def _():
        for tick in range(2):
            begun = pass_held.at[tick, pl.ds((1 - tick) * PARTS[0], tokens - (1 - tick) * PARTS[0])]
            remote(begun, begun, pass_sent.at[tick], pass_sem.at[0], (after, rank)).wait_send()


def body(n_pipe, stream, entering, gains, keys, values, weight):
    ticks, _, tokens, width = keys.shape
    piece = stream.shape[2]
    third = piece // N_ORDERS
    n = len(PARTS)
    slots = N_SENT * N_ORDERS
    vmem, dma = pltpu.VMEM, pltpu.SemaphoreType.DMA
    return pl.pallas_call(
        functools.partial(kernel, (n_pipe, ticks, tokens, width, piece)),
        out_shape=pltpu.VMEM((ticks, 1, tokens, piece), BF16),
        in_specs=[pl.BlockSpec(memory_space=pltpu.HBM)] * 6,
        out_specs=pl.BlockSpec(memory_space=pltpu.VMEM),
        scratch_shapes=[
            vmem((8 * N_ORDERS, width, third), BF16),
            vmem((ticks, tokens, width), BF16),
            vmem((ticks, tokens, width), BF16),
            vmem((ticks, tokens, piece), BF16),
            vmem((ticks, tokens, width), BF16),
            vmem((ticks, tokens, width), BF16),
            vmem((1, width), F32),
            vmem((ticks * tokens, width), BF16),
            vmem((slots, ticks * tokens, third), BF16),
            vmem((slots, ticks * tokens, third), BF16),
            vmem((ROUND_ROWS, piece), BF16),
            vmem((ticks * n, 8, 128), F32),
            vmem((8, ticks * n, 8, 128), F32),
            dma((8 * N_ORDERS,)),
            dma((5,)),
            dma((ticks * n, slots)),
            dma((slots,)),
            dma((ticks * n, 8)),
            dma((1,)),
            dma((ticks * n,)),
            dma((2, 2)),
            dma((ticks * n,)),
            dma((2,)),
            dma((n,)),
            dma((1,)),
            dma((1,)),
            dma((1,)),
        ],
        compiler_params=pltpu.CompilerParams(
            collective_id=0, has_side_effects=True, vmem_limit_bytes=62 * 2**20 + 400 * 2**10
        ),
        name="relay",
    )(stream, entering, gains, keys, values, weight)


def solution(mesh):
    in_specs = (
        P("pipe", None, "tensor"),
        P(None, None, "tensor"),
        P("pipe", None),
        P(None, "pipe", None, "tensor"),
        P(None, "pipe", None, "tensor"),
        P("pipe", "tensor", None),
    )
    out_specs = P(None, "pipe", None, "tensor")
    return jax.shard_map(
        functools.partial(body, mesh.shape["pipe"]),
        mesh=mesh, in_specs=in_specs, out_specs=out_specs, check_vma=False,
    )
```
